32 devices in a mesh: rep: 2 (over core), dp: 8 (over z, y), tensor: 2 (over x).
Axes of the slice: x: 2, y: 2, z: 4, core: 2. Of those that a mesh axis runs over, the one named last changes fastest.
Arguments:
- hidden_in: bfloat16 [8192, 8192], P(('rep', 'dp', 'tensor')), may hold values from -6 to 6
- queries: bfloat16 [8192, 8192], P(('rep', 'dp'), 'tensor'), may hold values from -6 to 6
- keys: bfloat16 [8192, 1024], P(('rep', 'dp'), 'tensor'), may hold values from -6 to 6
- values: bfloat16 [8192, 1024], P(('rep', 'dp'), 'tensor'), may hold values from -6 to 6
- out_grad: bfloat16 [8192, 8192], P(('rep', 'dp'), 'tensor'), may hold values from -6 to 6
- w_key: bfloat16 [8192, 1024], P('dp', 'tensor'), may hold values from -0.0625 to 0.0625
- w_value: bfloat16 [8192, 1024], P('dp', 'tensor'), may hold values from -0.0625 to 0.0625
- adam_state: float32 [2, 2, 8192, 1024], P(None, None, ('rep', 'dp'), 'tensor'), may hold values from -6 to 6
Outputs:
- query_grad: bfloat16 [8192, 8192], P(('rep', 'dp'), 'tensor')
- input_grad: bfloat16 [8192, 8192], P(('rep', 'dp', 'tensor'))
- key_weight_grad: float32 [8192, 1024], P(('rep', 'dp'), 'tensor')
- value_weight_grad: float32 [8192, 1024], P(('rep', 'dp'), 'tensor')
- state_backup: float32 [2, 2, 8192, 1024], P(None, None, ('rep', 'dp'), 'tensor')
The draws below stay inside these ranges and needn't reach their ends.
All inputs are finite; a program needn't handle non-finite values.
Results may differ from the reference program's by a relative error of at most 0.015.
Values may be sent and summed in bfloat16 or wider, within the bound.
A program may use at most 256 MiB of HBM per device.

```python
import math
import jax
import jax.numpy as jnp
from jax import lax

D = 8192
HEADS = 64
KVH = 8
HD = 128
LEN = 512
TOKENS = 8192
QW = 8192
KVW = 1024
N_TENSOR = 2


def draw_keys(key, part):
    key = jax.random.fold_in(key, 11)
    return jax.random.truncated_normal(key, -6.0, 6.0, (TOKENS, KVW), jnp.float32).astype(jnp.bfloat16)


def draw_queries(key, part):
    key = jax.random.fold_in(key, 12)
    return jax.random.truncated_normal(key, -6.0, 6.0, (TOKENS, QW), jnp.float32).astype(jnp.bfloat16)


def with_spikes(entries, rng, source, target, parts, factor):
    owner, partner = [(jnp.arange(entries.shape[axis_at]) // (entries.shape[axis_at] // parts)).reshape([-1 if axis == axis_at else 1 for axis in range(entries.ndim)]) for axis_at in (source, target)]
    chosen = jax.random.permutation(rng, parts)[partner]
    strong = (owner == chosen) | (owner == (partner + parts // 2) % parts)
    return jnp.where(strong, factor * entries, entries)


def shard_levels(stream_key, shape, split, smallest, top_value):
    factor_of, own = 1.0, jax.random.fold_in(stream_key, 6)
    for axis_at, blocks in split:
        steps = jnp.exp(jax.random.uniform(jax.random.fold_in(own, axis_at), (blocks,), jnp.float32, smallest / len(split), top_value / len(split)))
        factor_of = factor_of * jnp.repeat(steps, shape[axis_at] // blocks).reshape([-1 if axis == axis_at else 1 for axis in range(len(shape))])
    return factor_of


def scatter_about(key, dims, spread, bound, split=(), held_as=jnp.bfloat16):
    loudness = shard_levels(key, dims, split, -0.22, 0.18) if split else 1.0
    result = jax.random.normal(key, dims, jnp.float32) * spread * loudness
    return jnp.minimum(jnp.maximum(result, -bound), bound).astype(held_as)


def bell_draw_with(stream_key, dims, spread, limit, shards, heavy, dtype=jnp.bfloat16):
    result = spread * jax.random.normal(stream_key, dims, jnp.float32)
    if shards:
        result = result * shard_levels(stream_key, dims, shards, -0.22, 0.18)
    return jnp.clip(with_spikes(result, jax.random.fold_in(stream_key, 3), *heavy), -limit, limit).astype(dtype)


def setup_inputs(seed: int = 0) -> dict:
    key_of = jax.random.split(jax.random.key(seed), 9)
    hidden_in = bell_draw_with(key_of[0], (TOKENS, D), 1.0, 6.0, ((0, 32),), (0, 1, 32, 2.75))
    queries = draw_queries(jax.random.fold_in(key_of[8], 71), 0)
    keys = draw_keys(jax.random.fold_in(key_of[8], 71), 0)
    values = scatter_about(key_of[3], (TOKENS, KVW), 1.0, 6.0, ((0, 16), (1, 2)))
    out_grad = scatter_about(key_of[4], (TOKENS, QW), 1.0, 6.0, ((0, 16), (1, 2)))
    w_key = scatter_about(key_of[5], (D, KVW), D ** -0.5, 0.0625, ((0, 8), (1, 2)))
    w_value = scatter_about(key_of[6], (D, KVW), D ** -0.5, 0.0625, ((0, 8), (1, 2)))
    adam_state = scatter_about(key_of[7], (2, 2, D, KVW), 1.0, 6.0, ((2, 16), (3, 2)), jnp.float32)
    return dict(hidden_in=hidden_in, queries=queries, keys=keys, values=values, out_grad=out_grad, w_key=w_key, w_value=w_value, adam_state=adam_state)


def rope_tables(seq_len):
    positions = jnp.arange(seq_len).astype(jnp.float32)
    half_dim = HD // 2
    exponents = jnp.arange(half_dim).astype(jnp.float32) * (2.0 / HD)
    frequency = jnp.exp(-math.log(1000000.0) * exponents)
    angles = positions[:, None] * frequency[None, :]
    return (jnp.cos(angles), jnp.sin(angles))

def unrotate(gradient, cosine, sine_table):
    half_dim = HD // 2
    first_half = gradient[..., :half_dim]
    second_half = gradient[..., half_dim:]
    cos_wide = cosine[:, None, :]
    sin_wide = sine_table[:, None, :]
    return jnp.concatenate([first_half * cos_wide + second_half * sin_wide, second_half * cos_wide - first_half * sin_wide], axis=-1)

def sequence_grads(operands):
    query_seq, key_seq, value_seq, grad_seq = operands
    per_group = HEADS // KVH
    softmax_scale = 1.0 / math.sqrt(HD)
    high = lax.Precision.HIGHEST
    query_heads = query_seq.astype(jnp.float32).reshape(LEN, KVH, per_group, HD)
    grad_heads = grad_seq.astype(jnp.float32).reshape(LEN, KVH, per_group, HD)
    key_heads = key_seq.astype(jnp.float32).reshape(LEN, KVH, HD)
    value_heads = value_seq.astype(jnp.float32).reshape(LEN, KVH, HD)
    scores = jnp.einsum('qkgd,pkd->kgqp', query_heads, key_heads, precision=high) * softmax_scale
    positions = jnp.arange(LEN)
    allowed = positions[None, :] <= positions[:, None]
    scores = jnp.where(allowed, scores, -jnp.inf)
    row_top = lax.optimization_barrier(jnp.max(scores, axis=-1, keepdims=True))
    weights = jnp.exp(scores - row_top)
    probabilities = weights / lax.optimization_barrier(jnp.sum(weights, axis=-1, keepdims=True))
    probs_low = probabilities.astype(jnp.bfloat16).astype(jnp.float32)
    dprobs = jnp.einsum('qkgd,pkd->kgqp', grad_heads, value_heads, precision=high)
    delta = lax.optimization_barrier(jnp.sum(probabilities * dprobs, axis=-1, keepdims=True))
    dscores = (probabilities * (dprobs - delta) * softmax_scale).astype(jnp.bfloat16).astype(jnp.float32)
    query_grad = jnp.einsum('kgqp,pkd->qkgd', dscores, key_heads, precision=high)
    rotated = jnp.einsum('kgqp,qkgd->pkd', dscores, query_heads, precision=high)
    value_grad = jnp.einsum('kgqp,qkgd->pkd', probs_low, grad_heads, precision=high)
    cosine, sine_table = rope_tables(LEN)
    key_grad = unrotate(rotated, cosine, sine_table)
    return (query_grad.reshape(LEN, QW).astype(jnp.bfloat16), key_grad.reshape(LEN, KVW).astype(jnp.bfloat16), value_grad.reshape(LEN, KVW).astype(jnp.bfloat16))

def reference(hidden_in, queries, keys, values, out_grad, w_key, w_value, adam_state):
    seq_count = TOKENS // LEN
    operands = (queries.reshape(seq_count, LEN, QW), keys.reshape(seq_count, LEN, KVW), values.reshape(seq_count, LEN, KVW), out_grad.reshape(seq_count, LEN, QW))
    query_grad, key_grad, value_grad = lax.map(sequence_grads, operands)
    key_flat = key_grad.reshape(TOKENS, KVW)
    value_flat = value_grad.reshape(TOKENS, KVW)
    key_weight_grad = jnp.dot(hidden_in.T, key_flat, preferred_element_type=jnp.float32)
    value_weight_grad = jnp.dot(hidden_in.T, value_flat, preferred_element_type=jnp.float32)
    group_width = KVW // N_TENSOR

    def input_rows(pair):
        key_rows, value_rows = pair
        total = jnp.zeros((LEN, D), jnp.float32)
        for group_index in range(N_TENSOR):
            lower = group_index * group_width
            upper = lower + group_width
            term = jnp.dot(key_rows[:, lower:upper], w_key[:, lower:upper].T, preferred_element_type=jnp.float32)
            term = term + jnp.dot(value_rows[:, lower:upper], w_value[:, lower:upper].T, preferred_element_type=jnp.float32)
            total = total + lax.optimization_barrier(term.astype(jnp.bfloat16)).astype(jnp.float32)
        return total.astype(jnp.bfloat16)
    input_grad = lax.map(input_rows, (key_grad, value_grad)).reshape(TOKENS, D)
    half_rows = D // 2
    state_backup = jnp.concatenate([adam_state[:, :, half_rows:], adam_state[:, :, :half_rows]], axis=2)
    return (query_grad.reshape(TOKENS, QW), input_grad, key_weight_grad, value_weight_grad, state_backup)
```

```python
import functools
import math

import jax
import jax.numpy as jnp
import numpy as np
from jax import lax
from jax.experimental import pallas as pl
from jax.experimental.pallas import tpu as pltpu
from jax.sharding import PartitionSpec as P

HEADS = 64
KVH = 8
HD = 128
GROUP = HEADS // KVH
MESH = pl.DeviceIdType.MESH
F32, BF16 = jnp.float32, jnp.bfloat16
SUB = 512


def dot(a, b, dims):
    return lax.dot_general(a, b, (dims, ((), ())), preferred_element_type=F32)


def rope_tables(seq_len):
    half = HD // 2
    frequency = np.exp(-math.log(1000000.0) * np.arange(half) * (2.0 / HD))
    angles = np.arange(seq_len)[:, None] * frequency[None, :]
    cosine, sine = np.cos(angles), np.sin(angles)
    return (
        jnp.asarray(np.concatenate([cosine, cosine], 1), F32),
        jnp.asarray(np.concatenate([sine, -sine], 1), F32),
    )


def attention_kernel(q_ref, k_ref, v_ref, og_ref, cos_ref, sin_ref, qg_ref, kg_ref, vg_ref, kt_ref, vt_ref, k_sum, v_sum):
    seq = q_ref.shape[0]
    block = min(256, seq)
    scale = 1.0 / math.sqrt(HD)
    k = k_ref[...]
    v = v_ref[...]
    k_turned = k.T
    k_sum[...] = jnp.zeros_like(k_sum)
    v_sum[...] = jnp.zeros_like(v_sum)

    for head in range(GROUP):
        columns = pl.ds(head * HD, HD)
        for at in range(seq // block):
            rows = pl.ds(at * block, block)
            seen = (at + 1) * block
            q = q_ref[rows, columns]
            og = og_ref[rows, columns]
            scores = dot(k[:seen], q, ((1,), (1,)))
            key_at = lax.broadcasted_iota(jnp.int32, scores.shape, 0)
            query_at = lax.broadcasted_iota(jnp.int32, scores.shape, 1) + at * block
            scores = jnp.where(key_at <= query_at, scores, -jnp.inf)
            top = jnp.max(scores, axis=0, keepdims=True)
            weights = jnp.exp2((scores - top) * (scale * math.log2(math.e)))
            probs = weights * (1.0 / jnp.sum(weights, axis=0, keepdims=True))
            dprobs = dot(v[:seen], og, ((1,), (1,)))
            delta = jnp.sum(probs * dprobs, axis=0, keepdims=True)
            dscores = (probs * (dprobs - delta)).astype(BF16)
            turned = dot(k_turned[:, :seen], dscores, ((1,), (0,)))
            qg_ref[rows, columns] = (turned * scale).T.astype(BF16)
            k_sum[pl.ds(0, seen), :] += dot(dscores, q, ((1,), (0,)))
            v_sum[pl.ds(0, seen), :] += dot(probs.astype(BF16), og, ((1,), (0,)))

    r = k_sum[...] * scale
    kg = r * cos_ref[...] + pltpu.roll(r, HD // 2, 1) * sin_ref[...]
    vg = v_sum[...]
    kg_ref[...] = kg.astype(BF16)
    vg_ref[...] = vg.astype(BF16)
    kt_ref[...] = kg.T.astype(BF16)
    vt_ref[...] = vg.T.astype(BF16)


def attention_grads(queries, keys, values, out_grad):
    seq, width = queries.shape
    kv_width = keys.shape[1]
    groups = kv_width // HD
    cosine, sine = rope_tables(seq)
    wide = pl.BlockSpec((seq, GROUP * HD), lambda g: (0, g))
    narrow = pl.BlockSpec((seq, HD), lambda g: (0, g))
    turned = pl.BlockSpec((HD, seq), lambda g: (g, 0))
    table = pl.BlockSpec((seq, HD), lambda g: (0, 0))
    return pl.pallas_call(
        attention_kernel,
        grid=(groups,),
        in_specs=[wide, narrow, narrow, wide, table, table],
        out_specs=[wide, narrow, narrow, turned, turned],
        out_shape=[
            jax.ShapeDtypeStruct((seq, width), BF16),
            jax.ShapeDtypeStruct((seq, kv_width), BF16),
            jax.ShapeDtypeStruct((seq, kv_width), BF16),
            jax.ShapeDtypeStruct((kv_width, seq), BF16),
            jax.ShapeDtypeStruct((kv_width, seq), BF16),
        ],
        scratch_shapes=[pltpu.VMEM((seq, HD), F32), pltpu.VMEM((seq, HD), F32)],
        compiler_params=pltpu.CompilerParams(vmem_limit_bytes=40 * 2**20),
        cost_estimate=pl.CostEstimate(
            flops=10 * seq * seq * width,
            bytes_accessed=2 * (3 * seq * width + 6 * seq * kv_width),
            transcendentals=seq * seq * width // HD,
        ),
    )(queries, keys, values, out_grad, cosine, sine)


def tail_kernel(
    n_dp, n_tensor,
    kg_ref, vg_ref, kt_ref, vt_ref, hid_ref, w_ref,
    ig_ref, kw_ref, vw_ref, w_other,
    w_slots, hid_slots, ig_send, ig_recv, ig_own, a_send, a_recv, y_send, y_own, y_recv, z_recv, stage,
    w_sem, hid_sem, out_sem, wx_send_sem, wx_recv_sem, ig_send_sem, ig_recv_sem,
    a_send_sem, a_recv_sem, y_send_sem, y_recv_sem, z_send_sem, z_recv_sem,
):
    seq, width = kg_ref.shape
    model = hid_ref.shape[1]
    steps = n_dp // 2
    chunk = model // steps
    part = model // (2 * n_dp)
    sub = min(SUB, chunk)
    piece = seq // n_tensor
    r, d, t = lax.axis_index("rep"), lax.axis_index("dp"), lax.axis_index("tensor")
    a, b = d // 2, d % 2
    partner = {"rep": 1 - r}
    beside = {"dp": a * 2 + (1 - b)}

    def along(k):
        return {"dp": lax.rem(a + 1 + k, steps) * 2 + b}

    def across(k):
        return {"tensor": lax.rem(t + 1 + k, n_tensor)}

    peers = [partner, beside] + [along(k) for k in range(steps - 1)] + [across(k) for k in range(n_tensor - 1)]
    barrier = pltpu.get_barrier_semaphore()
    for peer in peers:
        pl.semaphore_signal(barrier, inc=1, device_id=peer, device_id_type=MESH)

    def send(src, dst, send_sem, recv_sem, peer):
        return pltpu.make_async_remote_copy(
            src_ref=src, dst_ref=dst, send_sem=send_sem, recv_sem=recv_sem, device_id=peer, device_id_type=MESH
        )

    def w_rows(i):
        return pl.ds(i * chunk, chunk)

    w_own = [pltpu.make_async_copy(w_ref.at[w_rows(i)], w_slots.at[i % 2, r], w_sem.at[0, i]) for i in range(steps)]
    w_got = [
        pltpu.make_async_copy(w_other.at[w_rows(i)], w_slots.at[i % 2, 1 - r], w_sem.at[1, i]) for i in range(steps)
    ]
    w_swap = [
        send(w_ref.at[w_rows(i)], w_other.at[w_rows(i)], wx_send_sem.at[i], wx_recv_sem.at[i], partner)
        for i in range(steps)
    ]

    def hid_copy(mine, i):
        owner = r if mine else 1 - r
        first = (owner * n_dp + lax.rem(a + 1 + i, steps) * 2) * part
        columns = pl.ds(pl.multiple_of(first, 2 * part), 2 * part)
        slot = int(mine)
        return pltpu.make_async_copy(hid_ref.at[:, columns], hid_slots.at[slot, i % 2], hid_sem.at[slot, i])

    hid_other = [hid_copy(False, i) for i in range(steps)]
    hid_mine = [hid_copy(True, i) for i in range(steps)]

    def a_copy(i):
        return send(a_send.at[i % 2], a_recv.at[i], a_send_sem.at[i], a_recv_sem.at[i], partner)

    def y_copy(i):
        return send(y_send.at[i], y_recv.at[i], y_send_sem.at[i], y_recv_sem.at[i], beside)

    def z_copy(i):
        return send(y_own.at[i], z_recv.at[i], z_send_sem.at[i], z_recv_sem.at[i], along(i))

    def ig_copy(i, k):
        return send(ig_send.at[k, i], ig_recv.at[k, i], ig_send_sem.at[k, i], ig_recv_sem.at[k, i], across(k))

    def turned_product(which, slot, which_b, half):
        turned = kt_ref if half == 0 else vt_ref
        columns = pl.ds(pl.multiple_of(which_b * part, part), part)
        return dot(turned[...], hid_slots[which, slot, :, columns], ((1,), (0,)))

    def input_grads(i):
        for s in range(chunk // sub):
            columns = pl.ds(s * sub, sub)
            total = dot(kg_ref[...], w_slots[i % 2, 0, columns, :], ((1,), (1,)))
            total = total + dot(vg_ref[...], w_slots[i % 2, 1, columns, :], ((1,), (1,)))
            stage[...] = total.astype(BF16)
            for k in range(n_tensor - 1):
                first = pl.multiple_of(lax.rem(t + 1 + k, n_tensor) * piece, piece)
                ig_send[k, i, :, columns] = stage[pl.ds(first, piece), :]
            ig_own[i, :, columns] = stage[pl.ds(pl.multiple_of(t * piece, piece), piece), :]

    def other_products(i):
        for which_b in range(2):
            for half in range(2):
                out = pl.ds(half * width, width)
                a_send[i % 2, which_b, out, :] = turned_product(0, i % 2, which_b, half).astype(BF16)

    def own_products(i, which_b, into):
        for half in range(2):
            out = pl.ds(half * width, width)
            total = turned_product(1, i % 2, which_b, half) + a_recv[i, which_b, out, :].astype(F32)
            into[i, out, :] = total.astype(BF16)

    w_own[0].start()
    hid_other[0].start()
    hid_mine[0].start()
    pl.semaphore_wait(barrier, len(peers))
    w_swap[0].start()

    for i in range(steps + 2):
        if i < steps:
            hid_other[i].wait()
            if i >= 2:
                a_copy(i - 2).wait_send()
            other_products(i)
            a_copy(i).start()
            if i + 1 < steps:
                w_swap[i + 1].start()
                hid_other[i + 1].start()
                w_own[i + 1].start()
            w_swap[i].wait_recv()
            w_got[i].start()
            w_got[i].wait()
            w_own[i].wait()
            input_grads(i)
            for k in range(n_tensor - 1):
                ig_copy(i, k).start()
        if 1 <= i <= steps:
            done = i - 1
            if i < steps:
                hid_mine[i].start()
            hid_mine[done].wait()
            a_copy(done).wait_recv()
            own_products(done, 1 - b, y_send)
            y_copy(done).start()
            own_products(done, b, y_own)
        if i >= 2:
            done = i - 2
            y_copy(done).wait_recv()
            if done < steps - 1:
                y_own[done] = (y_own[done].astype(F32) + y_recv[done].astype(F32)).astype(BF16)
                z_copy(done).start()

    ig_out = []
    for i in range(steps):
        for k in range(n_tensor - 1):
            ig_copy(i, k).wait_recv()
        for s in range(chunk // sub):
            columns = pl.ds(s * sub, sub)
            total = ig_own[i, :, columns].astype(F32)
            for k in range(n_tensor - 1):
                total = total + ig_recv[k, i, :, columns].astype(F32)
            ig_own[i, :, columns] = total.astype(BF16)
        copy = pltpu.make_async_copy(ig_own.at[i], ig_ref.at[:, pl.ds(i * chunk, chunk)], out_sem.at[i])
        copy.start()
        ig_out.append(copy)

    for k in range(steps - 1):
        z_copy(k).wait_recv()
    for half, out_ref in enumerate((kw_ref, vw_ref)):
        out = pl.ds(half * width, width)
        total = y_own[steps - 1, out, :].astype(F32) + y_recv[steps - 1, out, :].astype(F32)
        for k in range(steps - 1):
            total = total + z_recv[k, out, :].astype(F32)
        out_ref[...] = total.T

    for i in range(steps):
        w_swap[i].wait_send()
        y_copy(i).wait_send()
        if i < steps - 1:
            z_copy(i).wait_send()
        if i >= steps - 2:
            a_copy(i).wait_send()
        for k in range(n_tensor - 1):
            ig_copy(i, k).wait_send()
        ig_out[i].wait()


def tail(mesh, kg, vg, kt, vt, hid, w_half):
    n_dp, n_tensor = mesh.shape["dp"], mesh.shape["tensor"]
    seq, width = kg.shape
    model = hid.shape[1]
    steps = n_dp // 2
    chunk = model // steps
    part = model // (2 * n_dp)
    piece = seq // n_tensor
    others = n_tensor - 1
    sems = pltpu.SemaphoreType.DMA
    vmem = pl.BlockSpec(memory_space=pltpu.VMEM)
    anywhere = pl.BlockSpec(memory_space=pl.ANY)
    return pl.pallas_call(
        functools.partial(tail_kernel, n_dp, n_tensor),
        in_specs=[vmem, vmem, vmem, vmem, anywhere, anywhere],
        out_specs=[anywhere, vmem, vmem, anywhere],
        out_shape=[
            jax.ShapeDtypeStruct((piece, model), BF16),
            jax.ShapeDtypeStruct((part, width), F32),
            jax.ShapeDtypeStruct((part, width), F32),
            jax.ShapeDtypeStruct((model, width), BF16),
        ],
        scratch_shapes=[
            pltpu.VMEM((2, 2, chunk, width), BF16),
            pltpu.VMEM((2, 2, seq, 2 * part), BF16),
            pltpu.VMEM((others, steps, piece, chunk), BF16),
            pltpu.VMEM((others, steps, piece, chunk), BF16),
            pltpu.VMEM((steps, piece, chunk), BF16),
            pltpu.VMEM((2, 2, 2 * width, part), BF16),
            pltpu.VMEM((steps, 2, 2 * width, part), BF16),
            pltpu.VMEM((steps, 2 * width, part), BF16),
            pltpu.VMEM((steps, 2 * width, part), BF16),
            pltpu.VMEM((steps, 2 * width, part), BF16),
            pltpu.VMEM((steps - 1, 2 * width, part), BF16),
            pltpu.VMEM((seq, min(SUB, chunk)), BF16),
            sems((2, steps)),
            sems((2, steps)),
            sems((steps,)),
            sems((steps,)),
            sems((steps,)),
            sems((others, steps)),
            sems((others, steps)),
            sems((steps,)),
            sems((steps,)),
            sems((steps,)),
            sems((steps,)),
            sems((steps - 1,)),
            sems((steps - 1,)),
        ],
        compiler_params=pltpu.CompilerParams(
            collective_id=0, has_side_effects=True, vmem_limit_bytes=62 * 2**20
        ),
        cost_estimate=pl.CostEstimate(
            flops=8 * seq * width * model, bytes_accessed=8 * model * width, transcendentals=0
        ),
    )(kg, vg, kt, vt, hid, w_half)[:3]


def on_device(mesh, hidden_in, queries, keys, values, out_grad, w_key, w_value, adam_state):
    state_backup = lax.ppermute(adam_state, "rep", [(0, 1), (1, 0)])
    hidden = lax.all_gather(hidden_in, "tensor", axis=0, tiled=True)
    w_mine = jnp.where(lax.axis_index("rep") == 0, w_key, w_value)
    w_half = lax.all_gather(w_mine, "dp", axis=0, tiled=True)
    query_grad, kg, vg, kt, vt = attention_grads(queries, keys, values, out_grad)
    input_grad, key_weight_grad, value_weight_grad = tail(mesh, kg, vg, kt, vt, hidden, w_half)
    return (query_grad, input_grad, key_weight_grad, value_weight_grad, state_backup)


def solution(mesh):
    return jax.shard_map(
        functools.partial(on_device, mesh),
        mesh=mesh,
        in_specs=(
            P(("rep", "dp", "tensor"), None),
            P(("rep", "dp"), "tensor"),
            P(("rep", "dp"), "tensor"),
            P(("rep", "dp"), "tensor"),
            P(("rep", "dp"), "tensor"),
            P("dp", "tensor"),
            P("dp", "tensor"),
            P(None, None, ("rep", "dp"), "tensor"),
        ),
        out_specs=(
            P(("rep", "dp"), "tensor"),
            P(("rep", "dp", "tensor"), None),
            P(("rep", "dp"), "tensor"),
            P(("rep", "dp"), "tensor"),
            P(None, None, ("rep", "dp"), "tensor"),
        ),
        check_vma=False,
    )
```

```python
import functools
import math

import jax
import jax.numpy as jnp
import numpy as np
from jax import lax
from jax.experimental import pallas as pl
from jax.experimental.pallas import tpu as pltpu
from jax.sharding import PartitionSpec as P

HEADS = 64
KVH = 8
HD = 128
GROUP = HEADS // KVH
MESH = pl.DeviceIdType.MESH
F32, BF16 = jnp.float32, jnp.bfloat16
SUB = 512


def dot(a, b, dims):
    return lax.dot_general(a, b, (dims, ((), ())), preferred_element_type=F32)


def rope_tables(seq_len):
    half = HD // 2
    frequency = np.exp(-math.log(1000000.0) * np.arange(half) * (2.0 / HD))
    angles = np.arange(seq_len)[:, None] * frequency[None, :]
    cosine, sine = np.cos(angles), np.sin(angles)
    return (
        jnp.asarray(np.concatenate([cosine, cosine], 1), F32),
        jnp.asarray(np.concatenate([sine, -sine], 1), F32),
    )


def attention_kernel(q_ref, k_ref, v_ref, og_ref, cos_ref, sin_ref, qg_ref, kg_ref, vg_ref, kt_ref, vt_ref, k_sum, v_sum):
    seq = q_ref.shape[0]
    block = min(256, seq)
    scale = 1.0 / math.sqrt(HD)
    k = k_ref[...]
    v = v_ref[...]
    k_turned = k.T
    k_sum[...] = jnp.zeros_like(k_sum)
    v_sum[...] = jnp.zeros_like(v_sum)

    for head in range(GROUP):
        columns = pl.ds(head * HD, HD)
        for at in range(seq // block):
            rows = pl.ds(at * block, block)
            seen = (at + 1) * block
            q = q_ref[rows, columns]
            og = og_ref[rows, columns]
            scores = dot(k[:seen], q, ((1,), (1,)))
            key_at = lax.broadcasted_iota(jnp.int32, scores.shape, 0)
            query_at = lax.broadcasted_iota(jnp.int32, scores.shape, 1) + at * block
            scores = jnp.where(key_at <= query_at, scores, -jnp.inf)
            top = jnp.max(scores, axis=0, keepdims=True)
            weights = jnp.exp2((scores - top) * (scale * math.log2(math.e)))
            probs = weights * (1.0 / jnp.sum(weights, axis=0, keepdims=True))
            dprobs = dot(v[:seen], og, ((1,), (1,)))
            delta = jnp.sum(probs * dprobs, axis=0, keepdims=True)
            dscores = (probs * (dprobs - delta)).astype(BF16)
            turned = dot(k_turned[:, :seen], dscores, ((1,), (0,)))
            qg_ref[rows, columns] = (turned * scale).T.astype(BF16)
            k_sum[pl.ds(0, seen), :] += dot(dscores, q, ((1,), (0,)))
            v_sum[pl.ds(0, seen), :] += dot(probs.astype(BF16), og, ((1,), (0,)))

    r = k_sum[...] * scale
    kg = r * cos_ref[...] + pltpu.roll(r, HD // 2, 1) * sin_ref[...]
    vg = v_sum[...]
    kg_ref[...] = kg.astype(BF16)
    vg_ref[...] = vg.astype(BF16)
    kt_ref[...] = kg.T.astype(BF16)
    vt_ref[...] = vg.T.astype(BF16)


def attention_grads(queries, keys, values, out_grad):
    seq, width = queries.shape
    kv_width = keys.shape[1]
    groups = kv_width // HD
    cosine, sine = rope_tables(seq)
    wide = pl.BlockSpec((seq, GROUP * HD), lambda g: (0, g))
    narrow = pl.BlockSpec((seq, HD), lambda g: (0, g))
    turned = pl.BlockSpec((HD, seq), lambda g: (g, 0))
    table = pl.BlockSpec((seq, HD), lambda g: (0, 0))
    return pl.pallas_call(
        attention_kernel,
        grid=(groups,),
        in_specs=[wide, narrow, narrow, wide, table, table],
        out_specs=[wide, narrow, narrow, turned, turned],
        out_shape=[
            jax.ShapeDtypeStruct((seq, width), BF16),
            jax.ShapeDtypeStruct((seq, kv_width), BF16),
            jax.ShapeDtypeStruct((seq, kv_width), BF16),
            jax.ShapeDtypeStruct((kv_width, seq), BF16),
            jax.ShapeDtypeStruct((kv_width, seq), BF16),
        ],
        scratch_shapes=[pltpu.VMEM((seq, HD), F32), pltpu.VMEM((seq, HD), F32)],
        compiler_params=pltpu.CompilerParams(vmem_limit_bytes=62 * 2**20),
        cost_estimate=pl.CostEstimate(
            flops=10 * seq * seq * width,
            bytes_accessed=2 * (3 * seq * width + 6 * seq * kv_width),
            transcendentals=seq * seq * width // HD,
        ),
    )(queries, keys, values, out_grad, cosine, sine)


def by_distance(place, count, i):
    found = 0
    for here in range(count):
        near = sorted(range(count), key=lambda other: abs(other - here))
        found = found + jnp.where(place == here, near[i], 0)
    return found


def tail_kernel(
    n_dp, n_tensor, early,
    kg_ref, vg_ref, kt_ref, vt_ref, hid_ref, hid_early, w_ref, w_below, w_above, w_beside,
    ig_ref, kw_ref, vw_ref, w_all, hid_all,
    w_slots, hid_slots, ig_send, ig_recv, ig_own, a_send, a_recv, y_send, y_own, y_recv, z_recv, stage,
    w_sem, hid_sem, in_sem, out_sem,
    wz_send_sem, wz_recv_sem, wy_send_sem, wy_recv_sem, wr_send_sem, wr_recv_sem,
    hx_send_sem, hx_recv_sem, ig_send_sem, ig_recv_sem,
    a_send_sem, a_recv_sem, y_send_sem, y_recv_sem, z_send_sem, z_recv_sem,
):
    seq, width = kg_ref.shape
    model = hid_ref.shape[1]
    steps = n_dp // 2
    chunk = model // steps
    shard = model // n_dp
    part = model // (2 * n_dp)
    sub = min(SUB, chunk)
    piece = seq // n_tensor
    others = n_tensor - 1
    r, d, t = lax.axis_index("rep"), lax.axis_index("dp"), lax.axis_index("tensor")
    a, b = d // 2, d % 2
    partner = {"rep": 1 - r}
    beside = {"dp": a * 2 + (1 - b)}

    def along(k):
        return {"dp": lax.rem(a + 1 + k, steps) * 2 + b}

    def across(k):
        return {"tensor": lax.rem(t + 1 + k, n_tensor)}

    peers = [partner, beside] + [along(k) for k in range(steps - 1)] + [across(k) for k in range(others)]
    barrier = pltpu.get_barrier_semaphore()
    for peer in peers:
        pl.semaphore_signal(barrier, inc=1, device_id=peer, device_id_type=MESH)

    def send(src, dst, send_sem, recv_sem, peer):
        return pltpu.make_async_remote_copy(
            src_ref=src, dst_ref=dst, send_sem=send_sem, recv_sem=recv_sem, device_id=peer, device_id_type=MESH
        )

    near = [by_distance(a, steps, i) for i in range(steps)]

    def w_onward(i):
        place = near[i]
        target = jnp.where(place < a, a + 1, a - 1)
        inside = (target >= 0) & (target < steps)
        target = jnp.clip(target, 0, steps - 1)
        slot = w_all.at[r, place, b]
        return inside, send(slot, slot, wz_send_sem.at[place], wz_recv_sem.at[place], {"dp": target * 2 + b})

    def w_sideways(i):
        slot = w_all.at[r, near[i], b]
        return send(slot, slot, wy_send_sem.at[i], wy_recv_sem.at[i], beside)

    def w_swap(i, theirs):
        which = 1 - b if theirs else b
        slot = w_all.at[r, near[i], which]
        return send(slot, slot, wr_send_sem.at[i, int(theirs)], wr_recv_sem.at[i, int(theirs)], partner)

    def w_load(i):
        return [
            pltpu.make_async_copy(
                w_all.at[kind, near[i], which],
                w_slots.at[i % 2, kind, pl.ds(which * shard, shard)],
                w_sem.at[i, kind, which],
            )
            for kind in range(2)
            for which in range(2)
        ]

    def take_line(i):
        if i >= 1:

            @pl.when(jnp.abs(near[i] - a) >= 2)
            def _():
                w_onward(i)[1].wait_recv()

            inside, copy = w_onward(i)
            pl.when(inside)(copy.start)
            w_sideways(i).start()
        w_swap(i, False).start()

    def take_beside(i):
        if i >= 1:
            w_sideways(i).wait_recv()
        w_swap(i, True).start()

    def hid_columns(mine, i):
        owner = r if mine else 1 - r
        first = (owner * n_dp + lax.rem(a + 1 + i, steps) * 2) * part
        return pl.ds(pl.multiple_of(first, 2 * part), 2 * part)

    def hid_send(mine, i, k):
        w = int(mine)
        return send(
            hid_ref.at[:, hid_columns(mine, i)], hid_all.at[k, i, w], hx_send_sem.at[k, i, w], hx_recv_sem.at[k, i, w], across(k)
        )

    def hid_load(mine, i):
        w = int(mine)

        def rows(owner):
            return hid_slots.at[w, i % 2, pl.ds(pl.multiple_of(owner * piece, piece), piece)]

        copies = [pltpu.make_async_copy(hid_ref.at[:, hid_columns(mine, i)], rows(t), hid_sem.at[w, i, others])]
        for k in range(others):
            source = hid_early.at[k, i, w] if i < early else hid_all.at[k, i, w]
            owner = lax.rem(t + n_tensor - 1 - k, n_tensor)
            copies.append(pltpu.make_async_copy(source, rows(owner), hid_sem.at[w, i, k]))
        return copies

    def hid_start(mine, i):
        if i >= early:
            for k in range(others):
                hid_send(mine, i, k).wait_recv()
        for copy in hid_load(mine, i):
            copy.start()

    def hid_wait(mine, i):
        for copy in hid_load(mine, i):
            copy.wait()

    def a_copy(i):
        return send(a_send.at[i % 2], a_recv.at[i], a_send_sem.at[i], a_recv_sem.at[i], partner)

    def y_copy(i):
        return send(y_send.at[i], y_recv.at[i], y_send_sem.at[i], y_recv_sem.at[i], beside)

    def z_copy(i):
        return send(y_own.at[i], z_recv.at[i], z_send_sem.at[i], z_recv_sem.at[i], along(i))

    def ig_copy(i, k):
        return send(ig_send.at[k, i], ig_recv.at[k, i], ig_send_sem.at[k, i], ig_recv_sem.at[k, i], across(k))

    def turned_product(which, slot, which_b, half):
        turned = kt_ref if half == 0 else vt_ref
        columns = pl.ds(pl.multiple_of(which_b * part, part), part)
        return dot(turned[...], hid_slots[which, slot, :, columns], ((1,), (0,)))

    def input_grads(i):
        for s in range(chunk // sub):
            columns = pl.ds(s * sub, sub)
            total = dot(kg_ref[...], w_slots[i % 2, 0, columns, :], ((1,), (1,)))
            total = total + dot(vg_ref[...], w_slots[i % 2, 1, columns, :], ((1,), (1,)))
            stage[...] = total.astype(BF16)
            for k in range(n_tensor - 1):
                first = pl.multiple_of(lax.rem(t + 1 + k, n_tensor) * piece, piece)
                ig_send[k, i, :, columns] = stage[pl.ds(first, piece), :]
            ig_own[i, :, columns] = stage[pl.ds(pl.multiple_of(t * piece, piece), piece), :]

    def other_products(i):
        for which_b in range(2):
            for half in range(2):
                out = pl.ds(half * width, width)
                a_send[i % 2, which_b, out, :] = turned_product(0, i % 2, which_b, half).astype(BF16)

    def own_products(i, which_b, into):
        for half in range(2):
            out = pl.ds(half * width, width)
            total = turned_product(1, i % 2, which_b, half) + a_recv[i, which_b, out, :].astype(F32)
            into[i, out, :] = total.astype(BF16)

    def enter(index, source, place, which):
        return pltpu.make_async_copy(source, w_all.at[r, place, which], in_sem.at[index])

    below, above = jnp.maximum(a - 1, 0), jnp.minimum(a + 1, steps - 1)
    enter(0, w_ref, a, b).start()
    enter(1, w_beside, a, 1 - b).start()
    pl.when(a >= 1)(enter(2, w_below, below, b).start)
    pl.when(a + 1 < steps)(enter(3, w_above, above, b).start)
    pl.semaphore_wait(barrier, len(peers))
    for i in range(early, steps):
        for mine in (False, True):
            for k in range(others):
                hid_send(mine, i, k).start()
    enter(0, w_ref, a, b).wait()
    enter(1, w_beside, a, 1 - b).wait()
    pl.when(a >= 1)(enter(2, w_below, below, b).wait)
    pl.when(a + 1 < steps)(enter(3, w_above, above, b).wait)
    take_line(0)
    take_beside(0)
    take_line(1)

    for i in range(steps + 2):
        if i < steps:
            hid_start(False, i)
            if i >= 1:
                take_beside(i)
                if i + 1 < steps:
                    take_line(i + 1)
            hid_wait(False, i)
            if i >= 2:
                a_copy(i - 2).wait_send()
            other_products(i)
            a_copy(i).start()
            hid_start(True, i)
            w_swap(i, False).wait_recv()
            w_swap(i, True).wait_recv()
            for copy in w_load(i):
                copy.start()
        if 1 <= i <= steps:
            done = i - 1
            hid_wait(True, done)
            a_copy(done).wait_recv()
            own_products(done, 1 - b, y_send)
            y_copy(done).start()
            own_products(done, b, y_own)
        if i < steps:
            for copy in w_load(i):
                copy.wait()
            input_grads(i)
            for k in range(others):
                ig_copy(i, k).start()
        if i >= 2:
            done = i - 2
            y_copy(done).wait_recv()
            if done < steps - 1:
                y_own[done] = (y_own[done].astype(F32) + y_recv[done].astype(F32)).astype(BF16)
                z_copy(done).start()

    ig_out = []
    for i in range(steps):
        for k in range(n_tensor - 1):
            ig_copy(i, k).wait_recv()
        for s in range(chunk // sub):
            columns = pl.ds(s * sub, sub)
            total = ig_own[i, :, columns].astype(F32)
            for k in range(n_tensor - 1):
                total = total + ig_recv[k, i, :, columns].astype(F32)
            ig_own[i, :, columns] = total.astype(BF16)
        copy = pltpu.make_async_copy(ig_own.at[i], ig_ref.at[:, pl.ds(pl.multiple_of(near[i] * chunk, chunk), chunk)], out_sem.at[i])
        copy.start()
        ig_out.append(copy)

    for k in range(steps - 1):
        z_copy(k).wait_recv()
    for half, out_ref in enumerate((kw_ref, vw_ref)):
        out = pl.ds(half * width, width)
        total = y_own[steps - 1, out, :].astype(F32) + y_recv[steps - 1, out, :].astype(F32)
        for k in range(steps - 1):
            total = total + z_recv[k, out, :].astype(F32)
        out_ref[...] = total.T

    for i in range(steps):
        w_swap(i, False).wait_send()
        w_swap(i, True).wait_send()
        if i >= 1:
            inside, copy = w_onward(i)
            pl.when(inside)(copy.wait_send)
            w_sideways(i).wait_send()
        if i >= early:
            for mine in (False, True):
                for k in range(others):
                    hid_send(mine, i, k).wait_send()
        y_copy(i).wait_send()
        if i < steps - 1:
            z_copy(i).wait_send()
        if i >= steps - 2:
            a_copy(i).wait_send()
        for k in range(n_tensor - 1):
            ig_copy(i, k).wait_send()
        ig_out[i].wait()


EARLY = 1


def tail(mesh, kg, vg, kt, vt, hidden, hid_early, w_mine, w_below, w_above, w_beside):
    n_dp, n_tensor = mesh.shape["dp"], mesh.shape["tensor"]
    seq, width = kg.shape
    model = hidden.shape[1]
    steps = n_dp // 2
    chunk = model // steps
    shard = model // n_dp
    part = model // (2 * n_dp)
    piece = seq // n_tensor
    others = n_tensor - 1
    sems = pltpu.SemaphoreType.DMA
    vmem = pl.BlockSpec(memory_space=pltpu.VMEM)
    anywhere = pl.BlockSpec(memory_space=pl.ANY)
    return pl.pallas_call(
        functools.partial(tail_kernel, n_dp, n_tensor, EARLY),
        in_specs=[vmem] * 4 + [anywhere] * 6,
        out_specs=[anywhere, vmem, vmem, anywhere, anywhere],
        out_shape=[
            jax.ShapeDtypeStruct((piece, model), BF16),
            jax.ShapeDtypeStruct((part, width), F32),
            jax.ShapeDtypeStruct((part, width), F32),
            jax.ShapeDtypeStruct((2, steps, 2, shard, width), BF16),
            jax.ShapeDtypeStruct((others, steps, 2, piece, 2 * part), BF16),
        ],
        scratch_shapes=[
            pltpu.VMEM((2, 2, chunk, width), BF16),
            pltpu.VMEM((2, 2, seq, 2 * part), BF16),
            pltpu.VMEM((others, steps, piece, chunk), BF16),
            pltpu.VMEM((others, steps, piece, chunk), BF16),
            pltpu.VMEM((steps, piece, chunk), BF16),
            pltpu.VMEM((2, 2, 2 * width, part), BF16),
            pltpu.VMEM((steps, 2, 2 * width, part), BF16),
            pltpu.VMEM((steps, 2 * width, part), BF16),
            pltpu.VMEM((steps, 2 * width, part), BF16),
            pltpu.VMEM((steps, 2 * width, part), BF16),
            pltpu.VMEM((steps - 1, 2 * width, part), BF16),
            pltpu.VMEM((seq, min(SUB, chunk)), BF16),
            sems((steps, 2, 2)),
            sems((2, steps, n_tensor)),
            sems((4,)),
            sems((steps,)),
            sems((steps,)),
            sems((steps,)),
            sems((steps,)),
            sems((steps,)),
            sems((steps, 2)),
            sems((steps, 2)),
            sems((others, steps, 2)),
            sems((others, steps, 2)),
            sems((others, steps)),
            sems((others, steps)),
            sems((steps,)),
            sems((steps,)),
            sems((steps,)),
            sems((steps,)),
            sems((steps - 1,)),
            sems((steps - 1,)),
        ],
        compiler_params=pltpu.CompilerParams(
            collective_id=0, has_side_effects=True, vmem_limit_bytes=62 * 2**20
        ),
        cost_estimate=pl.CostEstimate(
            flops=8 * seq * width * model, bytes_accessed=8 * model * width, transcendentals=0
        ),
    )(kg, vg, kt, vt, hidden, hid_early, w_mine, w_below, w_above, w_beside)[:3]


def on_device(mesh, hidden_in, queries, keys, values, out_grad, w_key, w_value, adam_state):
    n_dp, n_tensor = mesh.shape["dp"], mesh.shape["tensor"]
    steps = n_dp // 2
    part = hidden_in.shape[1] // (2 * n_dp)
    r, a = lax.axis_index("rep"), lax.axis_index("dp") // 2

    early = []
    for i in range(EARLY):
        for owner in (1 - r, r):
            first = (owner * n_dp + (a + 1 + i) % steps * 2) * part
            early.append(lax.dynamic_slice_in_dim(hidden_in, first, 2 * part, 1))
    early = jnp.stack(early).reshape(EARLY, 2, -1, 2 * part)
    hid_early = jnp.stack(
        [
            lax.ppermute(early, "tensor", [(t, (t + 1 + k) % n_tensor) for t in range(n_tensor)])
            for k in range(n_tensor - 1)
        ]
    )

    w_mine = jnp.where(r == 0, w_key, w_value)
    w_beside = lax.ppermute(w_mine, "dp", [(d, d ^ 1) for d in range(n_dp)])
    w_below = lax.ppermute(w_mine, "dp", [(d, d + 2) for d in range(n_dp - 2)])
    w_above = lax.ppermute(w_mine, "dp", [(d + 2, d) for d in range(n_dp - 2)])
    state_backup = lax.ppermute(adam_state, "rep", [(0, 1), (1, 0)])

    query_grad, kg, vg, kt, vt = attention_grads(queries, keys, values, out_grad)
    input_grad, key_weight_grad, value_weight_grad = tail(
        mesh, kg, vg, kt, vt, hidden_in, hid_early, w_mine, w_below, w_above, w_beside
    )
    return (query_grad, input_grad, key_weight_grad, value_weight_grad, state_backup)


def solution(mesh):
    return jax.shard_map(
        functools.partial(on_device, mesh),
        mesh=mesh,
        in_specs=(
            P(("rep", "dp", "tensor"), None),
            P(("rep", "dp"), "tensor"),
            P(("rep", "dp"), "tensor"),
            P(("rep", "dp"), "tensor"),
            P(("rep", "dp"), "tensor"),
            P("dp", "tensor"),
            P("dp", "tensor"),
            P(None, None, ("rep", "dp"), "tensor"),
        ),
        out_specs=(
            P(("rep", "dp"), "tensor"),
            P(("rep", "dp", "tensor"), None),
            P(("rep", "dp"), "tensor"),
            P(("rep", "dp"), "tensor"),
            P(None, None, ("rep", "dp"), "tensor"),
        ),
        check_vma=False,
    )
```

```python
import functools
import math

import jax
import jax.numpy as jnp
import numpy as np
from jax import lax
from jax.experimental import pallas as pl
from jax.experimental.pallas import tpu as pltpu
from jax.sharding import PartitionSpec as P

HEADS = 64
KVH = 8
HD = 128
GROUP = HEADS // KVH
MESH = pl.DeviceIdType.MESH
F32, BF16 = jnp.float32, jnp.bfloat16
SUB = 512


def dot(a, b, dims):
    return lax.dot_general(a, b, (dims, ((), ())), preferred_element_type=F32)


def rope_tables(seq_len):
    half = HD // 2
    frequency = np.exp(-math.log(1000000.0) * np.arange(half) * (2.0 / HD))
    angles = np.arange(seq_len)[:, None] * frequency[None, :]
    cosine, sine = np.cos(angles), np.sin(angles)
    return (
        jnp.asarray(np.concatenate([cosine, cosine], 1), F32),
        jnp.asarray(np.concatenate([sine, -sine], 1), F32),
    )


def attention_kernel(q_ref, k_ref, v_ref, og_ref, cos_ref, sin_ref, qg_ref, kg_ref, vg_ref, kt_ref, vt_ref, k_sum, v_sum):
    seq = q_ref.shape[0]
    block = min(256, seq)
    scale = 1.0 / math.sqrt(HD)
    k = k_ref[...]
    v = v_ref[...]
    k_turned = k.T
    k_sum[...] = jnp.zeros_like(k_sum)
    v_sum[...] = jnp.zeros_like(v_sum)

    for head in range(GROUP):
        columns = pl.ds(head * HD, HD)
        for at in range(seq // block):
            rows = pl.ds(at * block, block)
            seen = (at + 1) * block
            q = q_ref[rows, columns]
            og = og_ref[rows, columns]
            scores = dot(k[:seen], q, ((1,), (1,)))
            key_at = lax.broadcasted_iota(jnp.int32, scores.shape, 0)
            query_at = lax.broadcasted_iota(jnp.int32, scores.shape, 1) + at * block
            scores = jnp.where(key_at <= query_at, scores, -jnp.inf)
            top = jnp.max(scores, axis=0, keepdims=True)
            weights = jnp.exp2((scores - top) * (scale * math.log2(math.e)))
            probs = weights * (1.0 / jnp.sum(weights, axis=0, keepdims=True))
            dprobs = dot(v[:seen], og, ((1,), (1,)))
            delta = jnp.sum(probs * dprobs, axis=0, keepdims=True)
            dscores = (probs * (dprobs - delta)).astype(BF16)
            turned = dot(k_turned[:, :seen], dscores, ((1,), (0,)))
            qg_ref[rows, columns] = (turned * scale).T.astype(BF16)
            k_sum[pl.ds(0, seen), :] += dot(dscores, q, ((1,), (0,)))
            v_sum[pl.ds(0, seen), :] += dot(probs.astype(BF16), og, ((1,), (0,)))

    r = k_sum[...] * scale
    kg = r * cos_ref[...] + pltpu.roll(r, HD // 2, 1) * sin_ref[...]
    vg = v_sum[...]
    kg_ref[...] = kg.astype(BF16)
    vg_ref[...] = vg.astype(BF16)
    kt_ref[...] = kg.T.astype(BF16)
    vt_ref[...] = vg.T.astype(BF16)


def attention_grads(queries, keys, values, out_grad):
    seq, width = queries.shape
    kv_width = keys.shape[1]
    groups = kv_width // HD
    cosine, sine = rope_tables(seq)
    wide = pl.BlockSpec((seq, GROUP * HD), lambda g: (0, g))
    narrow = pl.BlockSpec((seq, HD), lambda g: (0, g))
    turned = pl.BlockSpec((HD, seq), lambda g: (g, 0))
    table = pl.BlockSpec((seq, HD), lambda g: (0, 0))
    return pl.pallas_call(
        attention_kernel,
        grid=(groups,),
        in_specs=[wide, narrow, narrow, wide, table, table],
        out_specs=[wide, narrow, narrow, turned, turned],
        out_shape=[
            jax.ShapeDtypeStruct((seq, width), BF16),
            jax.ShapeDtypeStruct((seq, kv_width), BF16),
            jax.ShapeDtypeStruct((seq, kv_width), BF16),
            jax.ShapeDtypeStruct((kv_width, seq), BF16),
            jax.ShapeDtypeStruct((kv_width, seq), BF16),
        ],
        scratch_shapes=[pltpu.VMEM((seq, HD), F32), pltpu.VMEM((seq, HD), F32)],
        compiler_params=pltpu.CompilerParams(vmem_limit_bytes=62 * 2**20),
        cost_estimate=pl.CostEstimate(
            flops=10 * seq * seq * width,
            bytes_accessed=2 * (3 * seq * width + 6 * seq * kv_width),
            transcendentals=seq * seq * width // HD,
        ),
    )(queries, keys, values, out_grad, cosine, sine)


def by_distance(place, count, i):
    found = 0
    for here in range(count):
        near = sorted(range(count), key=lambda other: abs(other - here))
        found = found + jnp.where(place == here, near[i], 0)
    return found


def tail_kernel(
    n_dp, n_tensor, early,
    kg_ref, vg_ref, kt_ref, vt_ref, hid_ref, hid_early, w_ref, w_below, w_above, w_beside,
    ig_ref, kw_ref, vw_ref, w_all, hid_all,
    w_slots, hid_slots, ig_send, ig_recv, ig_own, a_send, a_recv, y_send, y_own, y_recv, z_recv, stage,
    w_sem, hid_sem, in_sem, out_sem,
    wz_send_sem, wz_recv_sem, wy_send_sem, wy_recv_sem, wr_send_sem, wr_recv_sem,
    hx_send_sem, hx_recv_sem, ig_send_sem, ig_recv_sem,
    a_send_sem, a_recv_sem, y_send_sem, y_recv_sem, z_send_sem, z_recv_sem,
):
    seq, width = kg_ref.shape
    model = hid_ref.shape[1]
    steps = n_dp // 2
    chunk = model // steps
    shard = model // n_dp
    part = model // (2 * n_dp)
    sub = min(SUB, chunk)
    piece = seq // n_tensor
    others = n_tensor - 1
    r, d, t = lax.axis_index("rep"), lax.axis_index("dp"), lax.axis_index("tensor")
    a, b = d // 2, d % 2
    partner = {"rep": 1 - r}
    beside = {"dp": a * 2 + (1 - b)}

    def along(k):
        return {"dp": lax.rem(a + 1 + k, steps) * 2 + b}

    def across(k):
        return {"tensor": lax.rem(t + 1 + k, n_tensor)}

    peers = [partner, beside] + [along(k) for k in range(steps - 1)] + [across(k) for k in range(others)]
    barrier = pltpu.get_barrier_semaphore()
    for peer in peers:
        pl.semaphore_signal(barrier, inc=1, device_id=peer, device_id_type=MESH)

    def send(src, dst, send_sem, recv_sem, peer):
        return pltpu.make_async_remote_copy(
            src_ref=src, dst_ref=dst, send_sem=send_sem, recv_sem=recv_sem, device_id=peer, device_id_type=MESH
        )

    near = [by_distance(a, steps, i) for i in range(steps)]

    def w_onward(i):
        place = near[i]
        target = jnp.where(place < a, a + 1, a - 1)
        inside = (target >= 0) & (target < steps)
        target = jnp.clip(target, 0, steps - 1)
        slot = w_all.at[r, place, b]
        return inside, send(slot, slot, wz_send_sem.at[place], wz_recv_sem.at[place], {"dp": target * 2 + b})

    def w_sideways(i):
        slot = w_all.at[r, near[i], b]
        return send(slot, slot, wy_send_sem.at[i], wy_recv_sem.at[i], beside)

    def w_swap(i, theirs):
        which = 1 - b if theirs else b
        slot = w_all.at[r, near[i], which]
        return send(slot, slot, wr_send_sem.at[i, int(theirs)], wr_recv_sem.at[i, int(theirs)], partner)

    def w_load(i):
        return [
            pltpu.make_async_copy(
                w_all.at[kind, near[i], which],
                w_slots.at[i % 2, kind, pl.ds(which * shard, shard)],
                w_sem.at[i, kind, which],
            )
            for kind in range(2)
            for which in range(2)
        ]

    def away(i):
        return jnp.abs(near[i] - a)

    def take_line(i):
        if i >= 1:

            @pl.when(away(i) >= 2)
            def _():
                w_onward(i)[1].wait_recv()

            inside, copy = w_onward(i)
            pl.when(inside & (away(i) >= 2))(copy.start)
            w_sideways(i).start()
        w_swap(i, False).start()

    def take_beside(i):
        if i >= 1:
            w_sideways(i).wait_recv()
        w_swap(i, True).start()

    def hid_columns(mine, i):
        owner = r if mine else 1 - r
        first = (owner * n_dp + lax.rem(a + 1 + i, steps) * 2) * part
        return pl.ds(pl.multiple_of(first, 2 * part), 2 * part)

    def hid_send(mine, i, k):
        w = int(mine)
        return send(
            hid_ref.at[:, hid_columns(mine, i)], hid_all.at[k, i, w], hx_send_sem.at[k, i, w], hx_recv_sem.at[k, i, w], across(k)
        )

    def hid_load(mine, i):
        w = int(mine)

        def rows(owner):
            return hid_slots.at[w, i % 2, pl.ds(pl.multiple_of(owner * piece, piece), piece)]

        copies = [pltpu.make_async_copy(hid_ref.at[:, hid_columns(mine, i)], rows(t), hid_sem.at[w, i, others])]
        for k in range(others):
            source = hid_early.at[k, i, w] if i < early else hid_all.at[k, i, w]
            owner = lax.rem(t + n_tensor - 1 - k, n_tensor)
            copies.append(pltpu.make_async_copy(source, rows(owner), hid_sem.at[w, i, k]))
        return copies

    def hid_start(mine, i):
        if i >= early:
            for k in range(others):
                hid_send(mine, i, k).wait_recv()
                if i + 1 < steps:
                    hid_send(mine, i + 1, k).start()
        for copy in hid_load(mine, i):
            copy.start()

    def hid_wait(mine, i):
        for copy in hid_load(mine, i):
            copy.wait()

    def a_copy(i):
        return send(a_send.at[i % 2], a_recv.at[i], a_send_sem.at[i], a_recv_sem.at[i], partner)

    def y_copy(i):
        return send(y_send.at[i], y_recv.at[i], y_send_sem.at[i], y_recv_sem.at[i], beside)

    def z_copy(i):
        return send(y_own.at[i], z_recv.at[i], z_send_sem.at[i], z_recv_sem.at[i], along(i))

    def ig_copy(i, k):
        return send(ig_send.at[k, i], ig_recv.at[k, i], ig_send_sem.at[k, i], ig_recv_sem.at[k, i], across(k))

    def turned_product(which, slot, which_b, half):
        turned = kt_ref if half == 0 else vt_ref
        columns = pl.ds(pl.multiple_of(which_b * part, part), part)
        return dot(turned[...], hid_slots[which, slot, :, columns], ((1,), (0,)))

    def input_grads(i):
        for s in range(chunk // sub):
            columns = pl.ds(s * sub, sub)
            total = dot(kg_ref[...], w_slots[i % 2, 0, columns, :], ((1,), (1,)))
            total = total + dot(vg_ref[...], w_slots[i % 2, 1, columns, :], ((1,), (1,)))
            stage[...] = total.astype(BF16)
            for k in range(n_tensor - 1):
                first = pl.multiple_of(lax.rem(t + 1 + k, n_tensor) * piece, piece)
                ig_send[k, i, :, columns] = stage[pl.ds(first, piece), :]
            ig_own[i, :, columns] = stage[pl.ds(pl.multiple_of(t * piece, piece), piece), :]

    def other_products(i):
        for which_b in range(2):
            for half in range(2):
                out = pl.ds(half * width, width)
                a_send[i % 2, which_b, out, :] = turned_product(0, i % 2, which_b, half).astype(BF16)

    def own_products(i, which_b, into):
        for half in range(2):
            out = pl.ds(half * width, width)
            total = turned_product(1, i % 2, which_b, half) + a_recv[i, which_b, out, :].astype(F32)
            into[i, out, :] = total.astype(BF16)

    def enter(index, source, place, which):
        return pltpu.make_async_copy(source, w_all.at[r, place, which], in_sem.at[index])

    below, above = jnp.maximum(a - 1, 0), jnp.minimum(a + 1, steps - 1)
    enter(0, w_ref, a, b).start()
    enter(1, w_beside, a, 1 - b).start()
    pl.when(a >= 1)(enter(2, w_below, below, b).start)
    pl.when(a + 1 < steps)(enter(3, w_above, above, b).start)
    pl.semaphore_wait(barrier, len(peers))
    for mine in (False, True):
        for k in range(others):
            hid_send(mine, early, k).start()
    enter(0, w_ref, a, b).wait()
    enter(1, w_beside, a, 1 - b).wait()
    pl.when(a >= 1)(enter(2, w_below, below, b).wait)
    pl.when(a + 1 < steps)(enter(3, w_above, above, b).wait)
    for i in range(1, min(3, steps)):
        inside, copy = w_onward(i)
        pl.when(inside & (away(i) == 1))(copy.start)
    take_line(0)
    take_beside(0)
    take_line(1)

    def input_step(i):
        w_swap(i, False).wait_recv()
        w_swap(i, True).wait_recv()
        for copy in w_load(i):
            copy.start()
        for copy in w_load(i):
            copy.wait()
        input_grads(i)

    def input_send(i):
        for k in range(others):
            ig_copy(i, k).start()

    def along_step(i):
        y_copy(i).wait_recv()
        if i < steps - 1:
            y_own[i] = (y_own[i].astype(F32) + y_recv[i].astype(F32)).astype(BF16)
            z_copy(i).start()

    taken, made, summed = 1, 0, 0
    for i in range(steps):
        hid_start(False, i)
        hid_wait(False, i)
        if i >= 2:
            a_copy(i - 2).wait_send()
        other_products(i)
        a_copy(i).start()
        hid_start(True, i)
        if i % 2 == 0:
            input_step(made)
            made += 1
        hid_wait(True, i)
        a_copy(i).wait_recv()
        own_products(i, 1 - b, y_send)
        y_copy(i).start()
        own_products(i, b, y_own)
        if 1 <= i < steps - 1:
            take_line(i + 1)
        if i % 2 == 1:
            take_beside(taken)
            taken += 1
        if i >= 3:
            along_step(summed)
            summed += 1
    for i in range(made):
        input_send(i)
    while made < steps:
        if taken <= made:
            take_beside(taken)
            taken += 1
        input_step(made)
        input_send(made)
        made += 1
        if summed < steps:
            along_step(summed)
            summed += 1
    while summed < steps:
        along_step(summed)
        summed += 1

    ig_out = []
    for i in range(steps):
        for k in range(n_tensor - 1):
            ig_copy(i, k).wait_recv()
        for s in range(chunk // sub):
            columns = pl.ds(s * sub, sub)
            total = ig_own[i, :, columns].astype(F32)
            for k in range(n_tensor - 1):
                total = total + ig_recv[k, i, :, columns].astype(F32)
            ig_own[i, :, columns] = total.astype(BF16)
        copy = pltpu.make_async_copy(ig_own.at[i], ig_ref.at[:, pl.ds(pl.multiple_of(near[i] * chunk, chunk), chunk)], out_sem.at[i])
        copy.start()
        ig_out.append(copy)

    for k in range(steps - 1):
        z_copy(k).wait_recv()
    for half, out_ref in enumerate((kw_ref, vw_ref)):
        out = pl.ds(half * width, width)
        total = y_own[steps - 1, out, :].astype(F32) + y_recv[steps - 1, out, :].astype(F32)
        for k in range(steps - 1):
            total = total + z_recv[k, out, :].astype(F32)
        out_ref[...] = total.T

    for i in range(steps):
        w_swap(i, False).wait_send()
        w_swap(i, True).wait_send()
        if i >= 1:
            inside, copy = w_onward(i)
            pl.when(inside)(copy.wait_send)
            w_sideways(i).wait_send()
        if i >= early:
            for mine in (False, True):
                for k in range(others):
                    hid_send(mine, i, k).wait_send()
        y_copy(i).wait_send()
        if i < steps - 1:
            z_copy(i).wait_send()
        if i >= steps - 2:
            a_copy(i).wait_send()
        for k in range(n_tensor - 1):
            ig_copy(i, k).wait_send()
        ig_out[i].wait()


EARLY = 1


def tail(mesh, kg, vg, kt, vt, hidden, hid_early, w_mine, w_below, w_above, w_beside):
    n_dp, n_tensor = mesh.shape["dp"], mesh.shape["tensor"]
    seq, width = kg.shape
    model = hidden.shape[1]
    steps = n_dp // 2
    chunk = model // steps
    shard = model // n_dp
    part = model // (2 * n_dp)
    piece = seq // n_tensor
    others = n_tensor - 1
    sems = pltpu.SemaphoreType.DMA
    vmem = pl.BlockSpec(memory_space=pltpu.VMEM)
    anywhere = pl.BlockSpec(memory_space=pl.ANY)
    return pl.pallas_call(
        functools.partial(tail_kernel, n_dp, n_tensor, EARLY),
        in_specs=[vmem] * 4 + [anywhere] * 6,
        out_specs=[anywhere, vmem, vmem, anywhere, anywhere],
        out_shape=[
            jax.ShapeDtypeStruct((piece, model), BF16),
            jax.ShapeDtypeStruct((part, width), F32),
            jax.ShapeDtypeStruct((part, width), F32),
            jax.ShapeDtypeStruct((2, steps, 2, shard, width), BF16),
            jax.ShapeDtypeStruct((others, steps, 2, piece, 2 * part), BF16),
        ],
        scratch_shapes=[
            pltpu.VMEM((2, 2, chunk, width), BF16),
            pltpu.VMEM((2, 2, seq, 2 * part), BF16),
            pltpu.VMEM((others, steps, piece, chunk), BF16),
            pltpu.VMEM((others, steps, piece, chunk), BF16),
            pltpu.VMEM((steps, piece, chunk), BF16),
            pltpu.VMEM((2, 2, 2 * width, part), BF16),
            pltpu.VMEM((steps, 2, 2 * width, part), BF16),
            pltpu.VMEM((steps, 2 * width, part), BF16),
            pltpu.VMEM((steps, 2 * width, part), BF16),
            pltpu.VMEM((steps, 2 * width, part), BF16),
            pltpu.VMEM((steps - 1, 2 * width, part), BF16),
            pltpu.VMEM((seq, min(SUB, chunk)), BF16),
            sems((steps, 2, 2)),
            sems((2, steps, n_tensor)),
            sems((4,)),
            sems((steps,)),
            sems((steps,)),
            sems((steps,)),
            sems((steps,)),
            sems((steps,)),
            sems((steps, 2)),
            sems((steps, 2)),
            sems((others, steps, 2)),
            sems((others, steps, 2)),
            sems((others, steps)),
            sems((others, steps)),
            sems((steps,)),
            sems((steps,)),
            sems((steps,)),
            sems((steps,)),
            sems((steps - 1,)),
            sems((steps - 1,)),
        ],
        compiler_params=pltpu.CompilerParams(
            collective_id=0, has_side_effects=True, vmem_limit_bytes=62 * 2**20
        ),
        cost_estimate=pl.CostEstimate(
            flops=8 * seq * width * model, bytes_accessed=8 * model * width, transcendentals=0
        ),
    )(kg, vg, kt, vt, hidden, hid_early, w_mine, w_below, w_above, w_beside)[:3]


def on_device(mesh, hidden_in, queries, keys, values, out_grad, w_key, w_value, adam_state):
    n_dp, n_tensor = mesh.shape["dp"], mesh.shape["tensor"]
    steps = n_dp // 2
    part = hidden_in.shape[1] // (2 * n_dp)
    r, a = lax.axis_index("rep"), lax.axis_index("dp") // 2

    early = []
    for i in range(EARLY):
        for owner in (1 - r, r):
            first = (owner * n_dp + (a + 1 + i) % steps * 2) * part
            early.append(lax.dynamic_slice_in_dim(hidden_in, first, 2 * part, 1))
    early = jnp.stack(early).reshape(EARLY, 2, -1, 2 * part)
    hid_early = jnp.stack(
        [
            lax.ppermute(early, "tensor", [(t, (t + 1 + k) % n_tensor) for t in range(n_tensor)])
            for k in range(n_tensor - 1)
        ]
    )

    w_mine = jnp.where(r == 0, w_key, w_value)
    w_beside = lax.ppermute(w_mine, "dp", [(d, d ^ 1) for d in range(n_dp)])
    w_below = lax.ppermute(w_mine, "dp", [(d, d + 2) for d in range(n_dp - 2)])
    w_above = lax.ppermute(w_mine, "dp", [(d + 2, d) for d in range(n_dp - 2)])
    state_backup = lax.ppermute(adam_state, "rep", [(0, 1), (1, 0)])

    query_grad, kg, vg, kt, vt = attention_grads(queries, keys, values, out_grad)
    input_grad, key_weight_grad, value_weight_grad = tail(
        mesh, kg, vg, kt, vt, hidden_in, hid_early, w_mine, w_below, w_above, w_beside
    )
    return (query_grad, input_grad, key_weight_grad, value_weight_grad, state_backup)


def solution(mesh):
    return jax.shard_map(
        functools.partial(on_device, mesh),
        mesh=mesh,
        in_specs=(
            P(("rep", "dp", "tensor"), None),
            P(("rep", "dp"), "tensor"),
            P(("rep", "dp"), "tensor"),
            P(("rep", "dp"), "tensor"),
            P(("rep", "dp"), "tensor"),
            P("dp", "tensor"),
            P("dp", "tensor"),
            P(None, None, ("rep", "dp"), "tensor"),
        ),
        out_specs=(
            P(("rep", "dp"), "tensor"),
            P(("rep", "dp", "tensor"), None),
            P(("rep", "dp"), "tensor"),
            P(("rep", "dp"), "tensor"),
            P(None, None, ("rep", "dp"), "tensor"),
        ),
        check_vma=False,
    )
```

```python
import functools
import math

import jax
import jax.numpy as jnp
import numpy as np
from jax import lax
from jax.experimental import pallas as pl
from jax.experimental.pallas import tpu as pltpu
from jax.sharding import PartitionSpec as P

HEADS = 64
KVH = 8
HD = 128
GROUP = HEADS // KVH
MESH = pl.DeviceIdType.MESH
F32, BF16 = jnp.float32, jnp.bfloat16
SUB = 512


def dot(a, b, dims):
    return lax.dot_general(a, b, (dims, ((), ())), preferred_element_type=F32)


def rope_tables(seq_len):
    half = HD // 2
    frequency = np.exp(-math.log(1000000.0) * np.arange(half) * (2.0 / HD))
    angles = np.arange(seq_len)[:, None] * frequency[None, :]
    cosine, sine = np.cos(angles), np.sin(angles)
    return (
        jnp.asarray(np.concatenate([cosine, cosine], 1), F32),
        jnp.asarray(np.concatenate([sine, -sine], 1), F32),
    )


def attention_kernel(q_ref, k_ref, v_ref, og_ref, cos_ref, sin_ref, qg_ref, kg_ref, vg_ref, kt_ref, vt_ref, k_sum, v_sum):
    seq = q_ref.shape[0]
    block = min(256, seq)
    scale = 1.0 / math.sqrt(HD)
    k = k_ref[...]
    v = v_ref[...]
    k_turned = k.T
    k_sum[...] = jnp.zeros_like(k_sum)
    v_sum[...] = jnp.zeros_like(v_sum)

    for head in range(GROUP):
        columns = pl.ds(head * HD, HD)
        for at in range(seq // block):
            rows = pl.ds(at * block, block)
            seen = (at + 1) * block
            q = q_ref[rows, columns]
            og = og_ref[rows, columns]
            scores = dot(k[:seen], q, ((1,), (1,)))
            key_at = lax.broadcasted_iota(jnp.int32, scores.shape, 0)
            query_at = lax.broadcasted_iota(jnp.int32, scores.shape, 1) + at * block
            scores = jnp.where(key_at <= query_at, scores, -jnp.inf)
            top = jnp.max(scores, axis=0, keepdims=True)
            weights = jnp.exp2((scores - top) * (scale * math.log2(math.e)))
            probs = weights * (1.0 / jnp.sum(weights, axis=0, keepdims=True))
            dprobs = dot(v[:seen], og, ((1,), (1,)))
            delta = jnp.sum(probs * dprobs, axis=0, keepdims=True)
            dscores = (probs * (dprobs - delta)).astype(BF16)
            turned = dot(k_turned[:, :seen], dscores, ((1,), (0,)))
            qg_ref[rows, columns] = (turned * scale).T.astype(BF16)
            k_sum[pl.ds(0, seen), :] += dot(dscores, q, ((1,), (0,)))
            v_sum[pl.ds(0, seen), :] += dot(probs.astype(BF16), og, ((1,), (0,)))

    r = k_sum[...] * scale
    kg = r * cos_ref[...] + pltpu.roll(r, HD // 2, 1) * sin_ref[...]
    vg = v_sum[...]
    kg_ref[...] = kg.astype(BF16)
    vg_ref[...] = vg.astype(BF16)
    kt_ref[...] = kg.T.astype(BF16)
    vt_ref[...] = vg.T.astype(BF16)


def attention_grads(queries, keys, values, out_grad):
    seq, width = queries.shape
    kv_width = keys.shape[1]
    groups = kv_width // HD
    cosine, sine = rope_tables(seq)
    wide = pl.BlockSpec((seq, GROUP * HD), lambda g: (0, g))
    narrow = pl.BlockSpec((seq, HD), lambda g: (0, g))
    turned = pl.BlockSpec((HD, seq), lambda g: (g, 0))
    table = pl.BlockSpec((seq, HD), lambda g: (0, 0))
    return pl.pallas_call(
        attention_kernel,
        grid=(groups,),
        in_specs=[wide, narrow, narrow, wide, table, table],
        out_specs=[wide, narrow, narrow, turned, turned],
        out_shape=[
            jax.ShapeDtypeStruct((seq, width), BF16),
            jax.ShapeDtypeStruct((seq, kv_width), BF16),
            jax.ShapeDtypeStruct((seq, kv_width), BF16),
            jax.ShapeDtypeStruct((kv_width, seq), BF16),
            jax.ShapeDtypeStruct((kv_width, seq), BF16),
        ],
        scratch_shapes=[pltpu.VMEM((seq, HD), F32), pltpu.VMEM((seq, HD), F32)],
        compiler_params=pltpu.CompilerParams(vmem_limit_bytes=62 * 2**20),
        cost_estimate=pl.CostEstimate(
            flops=10 * seq * seq * width,
            bytes_accessed=2 * (3 * seq * width + 6 * seq * kv_width),
            transcendentals=seq * seq * width // HD,
        ),
    )(queries, keys, values, out_grad, cosine, sine)


def tail_kernel(
    n_dp, n_tensor,
    kg_ref, vg_ref, kt_ref, vt_ref, hid_ref, w_ref,
    ig_ref, kw_ref, vw_ref, w_other,
    w_slots, hid_slots, ig_send, ig_recv, ig_own, a_send, a_recv, y_send, y_own, y_recv, z_recv, stage,
    w_sem, hid_sem, out_sem, wx_send_sem, wx_recv_sem, ig_send_sem, ig_recv_sem,
    a_send_sem, a_recv_sem, y_send_sem, y_recv_sem, z_send_sem, z_recv_sem,
):
    seq, width = kg_ref.shape
    model = hid_ref.shape[1]
    steps = n_dp // 2
    chunk = model // steps
    part = model // (2 * n_dp)
    sub = min(SUB, chunk)
    piece = seq // n_tensor
    r, d, t = lax.axis_index("rep"), lax.axis_index("dp"), lax.axis_index("tensor")
    a, b = d // 2, d % 2
    partner = {"rep": 1 - r}
    beside = {"dp": a * 2 + (1 - b)}

    def along(k):
        return {"dp": lax.rem(a + 1 + k, steps) * 2 + b}

    def across(k):
        return {"tensor": lax.rem(t + 1 + k, n_tensor)}

    peers = [partner, beside] + [along(k) for k in range(steps - 1)] + [across(k) for k in range(n_tensor - 1)]
    barrier = pltpu.get_barrier_semaphore()
    for peer in peers:
        pl.semaphore_signal(barrier, inc=1, device_id=peer, device_id_type=MESH)

    def send(src, dst, send_sem, recv_sem, peer):
        return pltpu.make_async_remote_copy(
            src_ref=src, dst_ref=dst, send_sem=send_sem, recv_sem=recv_sem, device_id=peer, device_id_type=MESH
        )

    def w_rows(i):
        return pl.ds(i * chunk, chunk)

    w_own = [pltpu.make_async_copy(w_ref.at[w_rows(i)], w_slots.at[i % 2, r], w_sem.at[0, i]) for i in range(steps)]
    w_got = [
        pltpu.make_async_copy(w_other.at[w_rows(i)], w_slots.at[i % 2, 1 - r], w_sem.at[1, i]) for i in range(steps)
    ]
    w_swap = [
        send(w_ref.at[w_rows(i)], w_other.at[w_rows(i)], wx_send_sem.at[i], wx_recv_sem.at[i], partner)
        for i in range(steps)
    ]

    def hid_copy(mine, i):
        owner = r if mine else 1 - r
        first = (owner * n_dp + lax.rem(a + 1 + i, steps) * 2) * part
        columns = pl.ds(pl.multiple_of(first, 2 * part), 2 * part)
        slot = int(mine)
        return pltpu.make_async_copy(hid_ref.at[:, columns], hid_slots.at[slot, i % 2], hid_sem.at[slot, i])

    hid_other = [hid_copy(False, i) for i in range(steps)]
    hid_mine = [hid_copy(True, i) for i in range(steps)]

    def a_copy(i):
        return send(a_send.at[i % 2], a_recv.at[i], a_send_sem.at[i], a_recv_sem.at[i], partner)

    def y_copy(i):
        return send(y_send.at[i], y_recv.at[i], y_send_sem.at[i], y_recv_sem.at[i], beside)

    def z_copy(i):
        return send(y_own.at[i], z_recv.at[i], z_send_sem.at[i], z_recv_sem.at[i], along(i))

    def ig_copy(i, k):
        return send(ig_send.at[k, i], ig_recv.at[k, i], ig_send_sem.at[k, i], ig_recv_sem.at[k, i], across(k))

    def turned_product(which, slot, which_b, half):
        turned = kt_ref if half == 0 else vt_ref
        columns = pl.ds(pl.multiple_of(which_b * part, part), part)
        return dot(turned[...], hid_slots[which, slot, :, columns], ((1,), (0,)))

    def input_grads(i):
        for s in range(chunk // sub):
            columns = pl.ds(s * sub, sub)
            total = dot(kg_ref[...], w_slots[i % 2, 0, columns, :], ((1,), (1,)))
            total = total + dot(vg_ref[...], w_slots[i % 2, 1, columns, :], ((1,), (1,)))
            stage[...] = total.astype(BF16)
            for k in range(n_tensor - 1):
                first = pl.multiple_of(lax.rem(t + 1 + k, n_tensor) * piece, piece)
                ig_send[k, i, :, columns] = stage[pl.ds(first, piece), :]
            ig_own[i, :, columns] = stage[pl.ds(pl.multiple_of(t * piece, piece), piece), :]

    def other_products(i):
        for which_b in range(2):
            for half in range(2):
                out = pl.ds(half * width, width)
                a_send[i % 2, which_b, out, :] = turned_product(0, i % 2, which_b, half).astype(BF16)

    def own_products(i, which_b, into):
        for half in range(2):
            out = pl.ds(half * width, width)
            total = turned_product(1, i % 2, which_b, half) + a_recv[i, which_b, out, :].astype(F32)
            into[i, out, :] = total.astype(BF16)

    w_own[0].start()
    hid_other[0].start()
    hid_mine[0].start()
    pl.semaphore_wait(barrier, len(peers))
    w_swap[0].start()

    for i in range(steps + 2):
        if i < steps:
            hid_other[i].wait()
            if i >= 2:
                a_copy(i - 2).wait_send()
            other_products(i)
            a_copy(i).start()
            if i + 1 < steps:
                w_swap[i + 1].start()
                hid_other[i + 1].start()
                w_own[i + 1].start()
            w_swap[i].wait_recv()
            w_got[i].start()
            w_got[i].wait()
            w_own[i].wait()
            input_grads(i)
            for k in range(n_tensor - 1):
                ig_copy(i, k).start()
        if 1 <= i <= steps:
            done = i - 1
            if i < steps:
                hid_mine[i].start()
            hid_mine[done].wait()
            a_copy(done).wait_recv()
            own_products(done, 1 - b, y_send)
            y_copy(done).start()
            own_products(done, b, y_own)
        if i >= 2:
            done = i - 2
            y_copy(done).wait_recv()
            if done < steps - 1:
                y_own[done] = (y_own[done].astype(F32) + y_recv[done].astype(F32)).astype(BF16)
                z_copy(done).start()

    ig_out = []
    for i in range(steps):
        for k in range(n_tensor - 1):
            ig_copy(i, k).wait_recv()
        for s in range(chunk // sub):
            columns = pl.ds(s * sub, sub)
            total = ig_own[i, :, columns].astype(F32)
            for k in range(n_tensor - 1):
                total = total + ig_recv[k, i, :, columns].astype(F32)
            ig_own[i, :, columns] = total.astype(BF16)
        copy = pltpu.make_async_copy(ig_own.at[i], ig_ref.at[:, pl.ds(i * chunk, chunk)], out_sem.at[i])
        copy.start()
        ig_out.append(copy)

    for k in range(steps - 1):
        z_copy(k).wait_recv()
    for half, out_ref in enumerate((kw_ref, vw_ref)):
        out = pl.ds(half * width, width)
        total = y_own[steps - 1, out, :].astype(F32) + y_recv[steps - 1, out, :].astype(F32)
        for k in range(steps - 1):
            total = total + z_recv[k, out, :].astype(F32)
        out_ref[...] = total.T

    for i in range(steps):
        w_swap[i].wait_send()
        y_copy(i).wait_send()
        if i < steps - 1:
            z_copy(i).wait_send()
        if i >= steps - 2:
            a_copy(i).wait_send()
        for k in range(n_tensor - 1):
            ig_copy(i, k).wait_send()
        ig_out[i].wait()


def tail(mesh, kg, vg, kt, vt, hid, w_half):
    n_dp, n_tensor = mesh.shape["dp"], mesh.shape["tensor"]
    seq, width = kg.shape
    model = hid.shape[1]
    steps = n_dp // 2
    chunk = model // steps
    part = model // (2 * n_dp)
    piece = seq // n_tensor
    others = n_tensor - 1
    sems = pltpu.SemaphoreType.DMA
    vmem = pl.BlockSpec(memory_space=pltpu.VMEM)
    anywhere = pl.BlockSpec(memory_space=pl.ANY)
    return pl.pallas_call(
        functools.partial(tail_kernel, n_dp, n_tensor),
        in_specs=[vmem, vmem, vmem, vmem, anywhere, anywhere],
        out_specs=[anywhere, vmem, vmem, anywhere],
        out_shape=[
            jax.ShapeDtypeStruct((piece, model), BF16),
            jax.ShapeDtypeStruct((part, width), F32),
            jax.ShapeDtypeStruct((part, width), F32),
            jax.ShapeDtypeStruct((model, width), BF16),
        ],
        scratch_shapes=[
            pltpu.VMEM((2, 2, chunk, width), BF16),
            pltpu.VMEM((2, 2, seq, 2 * part), BF16),
            pltpu.VMEM((others, steps, piece, chunk), BF16),
            pltpu.VMEM((others, steps, piece, chunk), BF16),
            pltpu.VMEM((steps, piece, chunk), BF16),
            pltpu.VMEM((2, 2, 2 * width, part), BF16),
            pltpu.VMEM((steps, 2, 2 * width, part), BF16),
            pltpu.VMEM((steps, 2 * width, part), BF16),
            pltpu.VMEM((steps, 2 * width, part), BF16),
            pltpu.VMEM((steps, 2 * width, part), BF16),
            pltpu.VMEM((steps - 1, 2 * width, part), BF16),
            pltpu.VMEM((seq, min(SUB, chunk)), BF16),
            sems((2, steps)),
            sems((2, steps)),
            sems((steps,)),
            sems((steps,)),
            sems((steps,)),
            sems((others, steps)),
            sems((others, steps)),
            sems((steps,)),
            sems((steps,)),
            sems((steps,)),
            sems((steps,)),
            sems((steps - 1,)),
            sems((steps - 1,)),
        ],
        compiler_params=pltpu.CompilerParams(
            collective_id=0, has_side_effects=True, vmem_limit_bytes=62 * 2**20
        ),
        cost_estimate=pl.CostEstimate(
            flops=8 * seq * width * model, bytes_accessed=8 * model * width, transcendentals=0
        ),
    )(kg, vg, kt, vt, hid, w_half)[:3]


def on_device(mesh, hidden_in, queries, keys, values, out_grad, w_key, w_value, adam_state):
    state_backup = lax.ppermute(adam_state, "rep", [(0, 1), (1, 0)])
    n_tensor, t = mesh.shape["tensor"], lax.axis_index("tensor")
    piece = hidden_in.shape[0]
    hidden = jnp.zeros((n_tensor * piece, hidden_in.shape[1]), BF16)
    hidden = lax.dynamic_update_slice_in_dim(hidden, hidden_in, t * piece, 0)
    for k in range(1, n_tensor):
        got = lax.ppermute(hidden_in, "tensor", [(s, (s + k) % n_tensor) for s in range(n_tensor)])
        hidden = lax.dynamic_update_slice_in_dim(hidden, got, (t + n_tensor - k) % n_tensor * piece, 0)
    w_mine = jnp.where(lax.axis_index("rep") == 0, w_key, w_value)
    w_half = lax.all_gather(w_mine, "dp", axis=0, tiled=True)
    query_grad, kg, vg, kt, vt = attention_grads(queries, keys, values, out_grad)
    input_grad, key_weight_grad, value_weight_grad = tail(mesh, kg, vg, kt, vt, hidden, w_half)
    return (query_grad, input_grad, key_weight_grad, value_weight_grad, state_backup)


def solution(mesh):
    return jax.shard_map(
        functools.partial(on_device, mesh),
        mesh=mesh,
        in_specs=(
            P(("rep", "dp", "tensor"), None),
            P(("rep", "dp"), "tensor"),
            P(("rep", "dp"), "tensor"),
            P(("rep", "dp"), "tensor"),
            P(("rep", "dp"), "tensor"),
            P("dp", "tensor"),
            P("dp", "tensor"),
            P(None, None, ("rep", "dp"), "tensor"),
        ),
        out_specs=(
            P(("rep", "dp"), "tensor"),
            P(("rep", "dp", "tensor"), None),
            P(("rep", "dp"), "tensor"),
            P(("rep", "dp"), "tensor"),
            P(None, None, ("rep", "dp"), "tensor"),
        ),
        check_vma=False,
    )
```
